32 devices in a mesh: frame: 4 (over x, core), band: 8 (over z, y).
Axes of the slice: x: 2, y: 2, z: 4, core: 2. Of those that a mesh axis runs over, the one named last changes fastest.
Arguments:
- noisy_snapshot_stack: bfloat16 [4, 8, 180, 512], P('frame', 'band'), may hold values from -6 to 6
- gaussian_perturbation: bfloat16 [4, 8, 180, 512], P('frame', 'band'), may hold values from -6 to 6
- snapshot_noise_indices: int32 [4], P('frame'), may hold values from 0 to 3, each once
- partition_longitude_starts: int32 [4], P('frame'), may hold values from 0 to 59
- latitude_patch_tally: int32 [8], replicated, may hold values from 90 to 180
- normalizer_scaling: float32 [512], replicated, may hold values from 0.1 to 1.9
- head_score_scales: float32 [2, 8], replicated, may hold values from 0.5 to 100
- local_projection_matrices: bfloat16 [512, 1536], P(None, 'band'), may hold values from -0.25 to 0.25
- time_projection_matrices: bfloat16 [512, 1536], P(None, 'band'), may hold values from -0.25 to 0.25
- final_projection_matrices: bfloat16 [1024, 512], P(None, 'band'), may hold values from -0.1875 to 0.1875
Outputs:
- next_state: bfloat16 [4, 8, 180, 512], P('frame', 'band')
The draws below stay inside these ranges and needn't reach their ends.
Inputs may be any that keep to these rules, and one draw needn't show every extreme that they name: `snapshot_noise_indices`: each level index 0 to 3 belongs to exactly one frame.
All inputs are finite; a program needn't handle non-finite values.
Results may differ from the reference program's by a relative error of at most 0.0071.
Values may be sent and summed in bfloat16 or wider, within the bound.
No kernel may reach another device: no remote copies, remote signals or barrier semaphores. Data moves between devices by JAX's collectives and lax.ppermute only.
A program may use at most 64 MiB of HBM per device.

```python
import math
import jax
import jax.numpy as jnp
from jax import lax

PATCH_BREADTH = 512
HEADS = 8
HEAD_DIM = 64
LON = 180
WINDOW = 60
PRIOR_SNAPSHOTS = 3
RB = 1
FRAMES = 4
LAT = 8
NBANDS = 8


def draw_head_score_scales(key, part):
    spread = jax.random.uniform(key, (2, HEADS), jnp.float32)
    return 0.5 * jnp.exp(spread * jnp.log(8.0))


def set_ends(values, key, least, high):
    shape = values.shape
    spot = [jax.random.randint(jax.random.fold_in(key, axis), (), 0, shape[axis]) for axis in range(len(shape))]
    values = values.at[tuple(spot)].set(least)
    longest = shape.index(max(shape))
    spot[longest] = (spot[longest] + 1) % shape[longest]
    return values.at[tuple(spot)].set(high)


def block_scale(stream_key, shape, pieces, smallest, top_value):
    loudness = 1.0
    for position, parts in pieces:
        draws = jax.random.uniform(jax.random.fold_in(jax.random.fold_in(stream_key, 6), position), (parts,), jnp.float32, smallest / len(pieces), top_value / len(pieces))
        loudness = loudness * jnp.repeat(jnp.exp(draws), shape[position] // parts).reshape((-1,) + (1,) * (len(shape) - 1 - position))
    return loudness


def noise(own_key, dims, width, most, pieces=(), kind=jnp.bfloat16):
    loudness = block_scale(own_key, dims, pieces, -0.22, 0.18) if pieces else 1.0
    entries = jax.random.normal(own_key, dims, jnp.float32) * width * loudness
    return jnp.minimum(jnp.maximum(entries, -most), most).astype(kind)


def setup_inputs(seed: int = 0) -> dict:
    seeds = jax.random.split(jax.random.key(seed), 11)
    return {
        "noisy_snapshot_stack": noise(seeds[0], (FRAMES, LAT, LON, PATCH_BREADTH), 1.0, 6.0, ((0, 4), (1, 8))),
        "gaussian_perturbation": noise(seeds[1], (FRAMES, LAT, LON, PATCH_BREADTH), 1.0, 6.0, ((0, 4), (1, 8))),
        "snapshot_noise_indices": jax.random.permutation(seeds[2], FRAMES).astype(jnp.int32),
        "partition_longitude_starts": set_ends(jax.random.randint(seeds[3], (FRAMES,), 0, WINDOW), jax.random.fold_in(seeds[3], 1), 0, WINDOW - 1).astype(jnp.int32),
        "latitude_patch_tally": set_ends(jax.random.randint(seeds[4], (NBANDS,), LON * RB // 2, LON * RB + 1), jax.random.fold_in(seeds[4], 1), LON * RB // 2, LON * RB).astype(jnp.int32),
        "normalizer_scaling": jnp.clip(1.0 + 0.18 * jax.random.normal(seeds[5], (PATCH_BREADTH,), jnp.float32), 0.1, 1.9),
        "head_score_scales": draw_head_score_scales(jax.random.fold_in(seeds[10], 71), 0),
        "local_projection_matrices": noise(seeds[7], (PATCH_BREADTH, 3 * PATCH_BREADTH), PATCH_BREADTH ** -0.5, 0.25, ((1, 8),)),
        "time_projection_matrices": noise(seeds[8], (PATCH_BREADTH, 3 * PATCH_BREADTH), PATCH_BREADTH ** -0.5, 0.25, ((1, 8),)),
        "final_projection_matrices": noise(seeds[9], (2 * PATCH_BREADTH, PATCH_BREADTH), (2 * PATCH_BREADTH) ** -0.5, 0.1875, ((1, 8),)),
    }


epsilon = 1e-06
sigma_low = 0.1
sigma_high = 2.0
keep_share = 0.8
fresh_share = 0.6

def sigma_of(level):
    return sigma_low * jnp.power(sigma_high / sigma_low, (level.astype(jnp.float32) + 1.0) / FRAMES)

def unit_heads(content_vectors):
    shaped = content_vectors.reshape(content_vectors.shape[:-1] + (HEADS, HEAD_DIM))
    scale = lax.rsqrt(lax.optimization_barrier(jnp.mean(shaped * shaped, axis=-1, keepdims=True)) + epsilon)
    return (shaped * scale).reshape(content_vectors.shape)

def project(frame, weight):
    rows, lon, token_extent = frame.shape
    out = jnp.dot(frame.reshape(-1, token_extent), weight, preferred_element_type=jnp.float32)
    asking_vectors = unit_heads(out[:, :token_extent]).astype(jnp.bfloat16).reshape(rows, lon, token_extent)
    key = unit_heads(out[:, token_extent:2 * token_extent]).astype(jnp.bfloat16).reshape(rows, lon, token_extent)
    value = out[:, 2 * token_extent:].astype(jnp.bfloat16).reshape(rows, lon, token_extent)
    return (asking_vectors, key, value)

def local_patch_mixer(asking_vectors, fringe_lookup_vectors, fringe_content_vectors, fringe_present_flags, snapshot_longitude_shift, temper):
    rows, lon, token_extent = asking_vectors.shape
    wins = lon // WINDOW
    asking_vectors = jnp.roll(asking_vectors, -snapshot_longitude_shift, axis=1).reshape(rows, wins, WINDOW, HEADS, HEAD_DIM)
    fringe_lookup_vectors = jnp.roll(fringe_lookup_vectors, -snapshot_longitude_shift, axis=1).reshape(rows + 2, wins, WINDOW, HEADS, HEAD_DIM)
    fringe_content_vectors = jnp.roll(fringe_content_vectors, -snapshot_longitude_shift, axis=1).reshape(rows + 2, wins, WINDOW, HEADS, HEAD_DIM)
    fringe_present_flags = jnp.roll(fringe_present_flags, -snapshot_longitude_shift, axis=1).reshape(rows + 2, wins, WINDOW)
    lookup_vectors = jnp.concatenate([fringe_lookup_vectors[:-2], fringe_lookup_vectors[1:-1], fringe_lookup_vectors[2:]], axis=2)
    content_vectors = jnp.concatenate([fringe_content_vectors[:-2], fringe_content_vectors[1:-1], fringe_content_vectors[2:]], axis=2)
    permitted_mask = jnp.concatenate([fringe_present_flags[:-2], fringe_present_flags[1:-1], fringe_present_flags[2:]], axis=2)
    inner = jnp.arange(WINDOW)
    middle = jnp.arange(3 * WINDOW)
    itself = middle[None, :] == inner[:, None] + WINDOW
    permitted_mask = permitted_mask[:, :, None, None, :] | itself[None, None, None]
    scores = jnp.einsum('rwqhd,rwkhd->rwhqk', asking_vectors.astype(jnp.float32), lookup_vectors.astype(jnp.float32))
    scores = scores * (temper / math.sqrt(HEAD_DIM))[None, None, :, None, None]
    top = lax.optimization_barrier(jnp.max(jnp.where(permitted_mask, scores, -jnp.inf), axis=-1, keepdims=True))
    weights = jnp.where(permitted_mask, jnp.exp(scores - top), 0.0)
    probs = (weights / lax.optimization_barrier(jnp.sum(weights, axis=-1, keepdims=True))).astype(jnp.bfloat16)
    combined_result_field = jnp.einsum('rwhqk,rwkhd->rwqhd', probs.astype(jnp.float32), content_vectors.astype(jnp.float32))
    combined_result_field = combined_result_field.reshape(rows, lon, token_extent)
    return jnp.roll(combined_result_field, snapshot_longitude_shift, axis=1).astype(jnp.bfloat16)

def across_time_mixer(asking_vectors, lookup_vectors, content_vectors, permitted_mask, temper):
    count, token_extent = asking_vectors.shape
    span = lookup_vectors.shape[0]
    query_heads = asking_vectors.astype(jnp.float32).reshape(count, HEADS, HEAD_DIM)
    key_heads = lookup_vectors.astype(jnp.float32).reshape(span, count, HEADS, HEAD_DIM)
    value_heads = content_vectors.astype(jnp.float32).reshape(span, count, HEADS, HEAD_DIM)
    scores = jnp.einsum('thd,jthd->jht', query_heads, key_heads)
    scores = scores * (temper / math.sqrt(HEAD_DIM))[None, :, None]
    top = lax.optimization_barrier(jnp.max(jnp.where(permitted_mask, scores, -jnp.inf), axis=0, keepdims=True))
    weights = jnp.where(permitted_mask, jnp.exp(scores - top), 0.0)
    probs = (weights / lax.optimization_barrier(jnp.sum(weights, axis=0, keepdims=True))).astype(jnp.bfloat16)
    combined_result_field = jnp.einsum('jht,jthd->thd', probs.astype(jnp.float32), value_heads)
    return combined_result_field.reshape(count, token_extent).astype(jnp.bfloat16)

def reference(noisy_snapshot_stack, gaussian_perturbation, snapshot_noise_indices, partition_longitude_starts, latitude_patch_tally, normalizer_scaling, head_score_scales, local_projection_matrices, time_projection_matrices, final_projection_matrices):
    state_f = noisy_snapshot_stack.astype(jnp.float32)
    normed = (state_f * lax.rsqrt(lax.optimization_barrier(jnp.mean(state_f * state_f, axis=-1, keepdims=True)) + epsilon) * normalizer_scaling).astype(jnp.bfloat16)
    row_ids = jnp.arange(LAT).astype(jnp.int32)
    band_of = row_ids // RB
    inner = (row_ids % RB)[:, None] * LON + jnp.arange(LON).astype(jnp.int32)[None, :]
    band_ids = jnp.arange(NBANDS).astype(jnp.int32)
    band_count = lax.optimization_barrier(jnp.sum(jnp.where(band_of[:, None] == band_ids[None, :], latitude_patch_tally[None, :], 0), axis=1))
    valid = inner < band_count[:, None]
    fringe_present_flags = jnp.pad(valid, ((1, 1), (0, 0)))

    def space_frame(args):
        frame, snapshot_longitude_shift = args
        asking_vectors, key, value = project(frame, local_projection_matrices)
        fringe_lookup_vectors = jnp.pad(key, ((1, 1), (0, 0), (0, 0)))
        fringe_content_vectors = jnp.pad(value, ((1, 1), (0, 0), (0, 0)))
        return local_patch_mixer(asking_vectors, fringe_lookup_vectors, fringe_content_vectors, fringe_present_flags, snapshot_longitude_shift, head_score_scales[0])
    space_mix = lax.map(space_frame, (normed, partition_longitude_starts))
    temporal_queries, time_key, time_value = lax.map(lambda frame: project(frame, time_projection_matrices), normed)
    padding = jnp.zeros((PRIOR_SNAPSHOTS, LAT, LON, PATCH_BREADTH), jnp.bfloat16)
    keys_all = jnp.concatenate([padding, time_key], axis=0)
    values_all = jnp.concatenate([padding, time_value], axis=0)
    frame_ids = jnp.arange(FRAMES).astype(jnp.int32)

    def time_frame(args):
        asking_vectors, index = args
        lookup_vectors = lax.dynamic_slice_in_dim(keys_all, index, PRIOR_SNAPSHOTS + 1, 0)
        content_vectors = lax.dynamic_slice_in_dim(values_all, index, PRIOR_SNAPSHOTS + 1, 0)
        allowed_pair_flags = index - PRIOR_SNAPSHOTS + jnp.arange(PRIOR_SNAPSHOTS + 1).astype(jnp.int32) >= 0
        combined_result_field = across_time_mixer(asking_vectors.reshape(-1, PATCH_BREADTH), lookup_vectors.reshape(PRIOR_SNAPSHOTS + 1, -1, PATCH_BREADTH), content_vectors.reshape(PRIOR_SNAPSHOTS + 1, -1, PATCH_BREADTH), allowed_pair_flags[:, None, None], head_score_scales[1])
        return combined_result_field.reshape(LAT, LON, PATCH_BREADTH)
    time_mix = lax.map(time_frame, (temporal_queries, frame_ids))
    mixed = jnp.concatenate([space_mix, time_mix], axis=-1).reshape(-1, 2 * PATCH_BREADTH)
    update = jnp.dot(mixed, final_projection_matrices, preferred_element_type=jnp.float32).reshape(FRAMES, LAT, LON, PATCH_BREADTH)
    sigma = sigma_of(snapshot_noise_indices)[:, None, None, None]
    sigma_next = sigma_of(snapshot_noise_indices - 1)[:, None, None, None]
    denoised = state_f / (1.0 + sigma * sigma) + sigma * lax.rsqrt(1.0 + sigma * sigma) * update
    noise_f = gaussian_perturbation.astype(jnp.float32)
    stepped = denoised + sigma_next * (keep_share * (state_f - denoised) / sigma + fresh_share * noise_f)
    finished = (snapshot_noise_indices == 0)[:, None, None, None]
    return jnp.where(finished, sigma_high * noise_f, stepped).astype(jnp.bfloat16)
```

```python
import functools
import math

import jax
import jax.numpy as jnp
from jax import lax
from jax.experimental import pallas as pl
from jax.experimental.pallas import tpu as pltpu
from jax.sharding import PartitionSpec as P

HEADS = 8
HEAD_DIM = 64
WINDOW = 60
PRIOR_SNAPSHOTS = 3

epsilon = 1e-06
sigma_low = 0.1
sigma_high = 2.0
keep_share = 0.8
fresh_share = 0.6
LOG2E = 1.4426950408889634
FAR = -1e30

AXES = ("frame", "band")
BF = jnp.bfloat16
F32 = jnp.float32


def ring_band(pos, n):
    return jnp.where(pos < n // 2, 2 * pos, 2 * (n - 1 - pos) + 1)


def ring_pairs(nf, n):
    order = list(range(0, n, 2)) + list(range(1, n, 2))[::-1]
    pairs = []
    for f in range(nf):
        step = 1 if f % 2 == 0 else -1
        for p in range(n):
            pairs.append((f * n + order[p], f * n + order[(p + step) % n]))
    return pairs


def core_pairs(nf, n):
    return [(f * n + b, (f ^ 1) * n + b) for f in range(nf) for b in range(n)]


def shift_frame(block, hop):
    nf = lax.axis_size("frame")
    return lax.ppermute(block, "frame", [(i, i + hop) for i in range(nf - hop)])


def shift_band(block, hop):
    n = lax.axis_size("band")
    return lax.ppermute(block, "band", [(i, i + hop) for i in range(n) if 0 <= i + hop < n])


def unit_rows(block):
    shaped = block.reshape(HEADS, HEAD_DIM, block.shape[-1])
    mean = jnp.mean(shaped * shaped, axis=1, keepdims=True)
    return (shaped * lax.rsqrt(mean + epsilon)).reshape(block.shape)


def kernel(
    slots, n_time, n_bands, total_levels,
    meta, scales, tally, gain_ref, state_ref, noise_ref, *rest,
):
    space_refs = (state_ref,) + rest[:2]
    time_refs = (state_ref,) + rest[2 : 1 + n_time]
    rest = rest[1 + n_time :]
    first, second = rest[:slots], rest[slots : 2 * slots]
    out_ref = rest[2 * slots]
    weights, final, qs, ks, vs, mix = rest[2 * slots + 1 :]
    lon, width = state_ref.shape
    parity, shift, level = meta[slots], meta[slots + 1], meta[slots + 2]
    frame, band = meta[slots + 3], meta[slots + 4]
    r3 = 3 * width // n_bands
    r1 = width // n_bands

    for group, which in ((first, parity), (second, 1 - parity)):
        for i, ref in enumerate(group):
            b = meta[i]
            weights[which, pl.ds(pl.multiple_of(b * r3, 16), r3), :] = ref[0:r3, :]
            final[which, pl.ds(pl.multiple_of(b * r1, 16), r1), :] = ref[r3 : r3 + r1, :]

    def normed(ref):
        x = ref[...].astype(F32)
        scale = lax.rsqrt(jnp.mean(x * x, axis=-1, keepdims=True) + epsilon)
        return (x * scale * gain_ref[...]).astype(BF)

    nt = (((1,), (1,)), ((), ()))

    def proj(which, part, x):
        return lax.dot_general(
            weights[which, part * width : (part + 1) * width, :], x, nt, preferred_element_type=F32
        )

    own = normed(state_ref)
    qs[0] = unit_rows(proj(0, 0, own)).astype(BF)
    for j, ref in enumerate(space_refs):
        x = own if j == 0 else normed(ref)
        ks[j] = unit_rows(proj(0, 1, x)).astype(BF)
        vs[j] = proj(0, 2, x).astype(BF)
    qs[1] = unit_rows(proj(1, 0, own)).astype(BF)
    for j, ref in enumerate(time_refs):
        x = own if j == 0 else normed(ref)
        ks[3 + j] = unit_rows(proj(1, 1, x)).astype(BF)
        vs[3 + j] = proj(1, 2, x).astype(BF)

    kcol = lax.broadcasted_iota(jnp.int32, (lon, lon), 0)
    qcol = lax.broadcasted_iota(jnp.int32, (lon, lon), 1)

    def window(col):
        c = col - shift
        c = jnp.where(c < 0, c + lon, c)
        w = jnp.zeros_like(c)
        for edge in range(WINDOW, lon, WINDOW):
            w = w + (c >= edge).astype(jnp.int32)
        return w

    same = window(kcol) == window(qcol)
    biases = []
    for j, off in enumerate((0, -1, 1)):
        row = band + off
        exists = (row >= 0) & (row < n_bands)
        limit = jnp.where(exists, tally[jnp.clip(row, 0, n_bands - 1)], 0)
        seen = same & (kcol < limit)
        if j == 0:
            seen = seen | (kcol == qcol)
        biases.append(jnp.where(seen, 0.0, FAR).astype(F32))
    tn = (((0,), (0,)), ((), ()))
    for h in range(HEADS):
        lo = h * HEAD_DIM
        hi = lo + HEAD_DIM
        factor = scales[0, h] * (LOG2E / math.sqrt(HEAD_DIM))
        q = qs[0, lo:hi, :]
        x = [
            lax.dot_general(ks[j, lo:hi, :], q, tn, preferred_element_type=F32) * factor + biases[j]
            for j in range(3)
        ]
        top = jnp.max(jnp.maximum(jnp.maximum(x[0], x[1]), x[2]), axis=0, keepdims=True)
        e = [jnp.exp2(s - top) for s in x]
        inv = 1.0 / jnp.sum(e[0] + e[1] + e[2], axis=0, keepdims=True)
        o = sum(
            jnp.dot(vs[j, lo:hi, :], (e[j] * inv).astype(BF), preferred_element_type=F32)
            for j in range(3)
        )
        mix[0, lo:hi, :] = o.astype(BF)

    odd = frame % 2
    back = [0, 2, jnp.where(odd == 1, 1, -1), jnp.where(odd == 1, 3, 1), jnp.where(odd == 1, -1, 3)]
    allow = [(b >= 0) & (b <= PRIOR_SNAPSHOTS) & (frame - b >= 0) for b in back]
    shut = [jnp.where(a, 0.0, FAR).astype(F32) for a in allow]
    for h in range(HEADS):
        lo = h * HEAD_DIM
        hi = lo + HEAD_DIM
        factor = scales[1, h] * (LOG2E / math.sqrt(HEAD_DIM))
        q = qs[1, lo:hi, :].astype(F32)
        x = [
            jnp.sum(q * ks[3 + j, lo:hi, :].astype(F32), axis=0, keepdims=True) * factor + shut[j]
            for j in range(n_time)
        ]
        top = functools.reduce(jnp.maximum, x)
        e = [jnp.exp2(s - top) for s in x]
        inv = 1.0 / sum(e)
        o = sum(
            (e[j] * inv).astype(BF).astype(F32) * vs[3 + j, lo:hi, :].astype(F32)
            for j in range(n_time)
        )
        mix[1, lo:hi, :] = o.astype(BF)

    update = jnp.dot(final[0], mix[0], preferred_element_type=F32) + jnp.dot(
        final[1], mix[1], preferred_element_type=F32
    )
    update = update.T

    def sigma_of(lv):
        power = (jnp.full((1, width), lv, jnp.int32).astype(F32) + 1.0) / total_levels
        return sigma_low * jnp.exp(power * math.log(sigma_high / sigma_low))

    s, s_next = sigma_of(level), sigma_of(level - 1)
    state = state_ref[...].astype(F32)
    fresh = noise_ref[...].astype(F32)
    denoised = state / (1.0 + s * s) + s * lax.rsqrt(1.0 + s * s) * update
    stepped = denoised + s_next * (keep_share * (state - denoised) / s + fresh_share * fresh)
    out_ref[...] = jnp.where(level == 0, sigma_high * fresh, stepped).astype(BF)


def body(
    noisy_snapshot_stack,
    gaussian_perturbation,
    snapshot_noise_indices,
    partition_longitude_starts,
    latitude_patch_tally,
    normalizer_scaling,
    head_score_scales,
    local_projection_matrices,
    time_projection_matrices,
    final_projection_matrices,
):
    frames, rows, lon, width = noisy_snapshot_stack.shape
    assert frames == 1 and rows == 1
    n, nf = lax.axis_size("band"), lax.axis_size("frame")
    assert n % 2 == 0 and nf % 2 == 0
    band, frame = lax.axis_index("band"), lax.axis_index("frame")
    parity = frame % 2
    state = noisy_snapshot_stack.reshape(lon, width)
    noise = gaussian_perturbation.reshape(lon, width)

    chunk_a = jnp.concatenate([local_projection_matrices, final_projection_matrices[:width]], axis=1).T
    chunk_b = jnp.concatenate([time_projection_matrices, final_projection_matrices[width:]], axis=1).T
    own0 = jnp.where(parity == 0, chunk_a, chunk_b)
    own1 = jnp.where(parity == 0, chunk_b, chunk_a)

    ring, core = ring_pairs(nf, n), core_pairs(nf, n)
    half = n // 2
    chain0, chain1 = [own0], [own1]
    for h in range(half):
        chain0.append(lax.ppermute(chain0[-1], AXES, ring))
        if h < half - 1:
            chain1.append(lax.ppermute(chain1[-1], AXES, ring))
    swap0 = [lax.ppermute(c, AXES, core) for c in chain0[1:half]]
    swap1 = [lax.ppermute(c, AXES, core) for c in chain1[1:half]]
    swap_last = lax.ppermute(chain0[half], AXES, core)
    first = chain0 + swap1
    second = chain1 + [swap_last] + swap0

    above = shift_band(state, 1)
    below = shift_band(state, -1)
    two_back = shift_frame(state, 2)
    partner = lax.ppermute(state, AXES, core)
    partner_two = lax.ppermute(two_back, AXES, core)
    past = [two_back, partner, partner_two]
    if nf > 4:
        past.append(shift_frame(state, 3))

    pos = jnp.where(band % 2 == 0, band // 2, n - 1 - band // 2)
    away = jnp.array(list(range(0, -half - 1, -1)) + list(range(1, half)), jnp.int32)
    slot_pos = (pos + jnp.where(parity == 0, away, -away)) % n
    meta = jnp.concatenate(
        [
            ring_band(slot_pos, n),
            jnp.stack(
                [parity, partition_longitude_starts[0], snapshot_noise_indices[0], frame, band]
            ),
        ]
    ).astype(jnp.int32)

    smem = pl.BlockSpec(memory_space=pltpu.SMEM)
    vmem = pl.BlockSpec(memory_space=pltpu.VMEM)
    operands = [state, noise, above, below] + past + first + second
    n_time = 1 + len(past)
    out = pl.pallas_call(
        functools.partial(kernel, n, n_time, n, nf),
        out_shape=jax.ShapeDtypeStruct((lon, width), BF),
        in_specs=[smem] * 3 + [vmem] * (1 + len(operands)),
        out_specs=vmem,
        scratch_shapes=[
            pltpu.VMEM((2, 3 * width, width), BF),
            pltpu.VMEM((2, width, width), BF),
            pltpu.VMEM((2, width, lon), BF),
            pltpu.VMEM((3 + n_time, width, lon), BF),
            pltpu.VMEM((3 + n_time, width, lon), BF),
            pltpu.VMEM((2, width, lon), BF),
        ],
        compiler_params=pltpu.CompilerParams(vmem_limit_bytes=40 * 1024 * 1024),
    )(meta, head_score_scales, latitude_patch_tally, normalizer_scaling.reshape(1, width), *operands)
    return out.reshape(noisy_snapshot_stack.shape)


def solution(mesh):
    return jax.shard_map(
        body,
        mesh=mesh,
        in_specs=(
            P("frame", "band", None, None),
            P("frame", "band", None, None),
            P("frame"),
            P("frame"),
            P(),
            P(),
            P(),
            P(None, "band"),
            P(None, "band"),
            P(None, "band"),
        ),
        out_specs=P("frame", "band", None, None),
        check_vma=False,
    )
```

```python
import functools
import math

import jax
import jax.numpy as jnp
from jax import lax
from jax.experimental import pallas as pl
from jax.experimental.pallas import tpu as pltpu
from jax.sharding import PartitionSpec as P

HEADS = 8
HEAD_DIM = 64
WINDOW = 60
PRIOR_SNAPSHOTS = 3

epsilon = 1e-06
sigma_low = 0.1
sigma_high = 2.0
keep_share = 0.8
fresh_share = 0.6
LOG2E = 1.4426950408889634
FAR = -1e30
TIE = 9
LARGE = 60 * 1024 * 1024

AXES = ("frame", "band")
BF = jnp.bfloat16
F32 = jnp.float32


def slot_bands(band, parity, n):
    even = lax.rem(band, 2) == 0
    pos = jnp.where(even, band // 2, n - 1 - band // 2)
    half = n // 2
    bands = []
    for away in [*range(0, half + 1), *range(-1, -half, -1)]:
        p = lax.rem(pos + jnp.where(parity == 0, n - away, n + away), n)
        bands.append(jnp.where(p < half, 2 * p, 2 * (n - 1 - p) + 1))
    return bands


def ring_pairs(nf, n):
    order = list(range(0, n, 2)) + list(range(1, n, 2))[::-1]
    pairs = []
    for f in range(nf):
        step = 1 if f % 2 == 0 else -1
        for p in range(n):
            pairs.append((f * n + order[p], f * n + order[(p + step) % n]))
    return pairs


def core_pairs(nf, n, first=0, stride=1):
    return [(f * n + b, (f ^ 1) * n + b) for f in range(first, nf, stride) for b in range(n)]


def rotate_frame(block, hop):
    nf = lax.axis_size("frame")
    return lax.ppermute(block, "frame", [(i, (i + hop) % nf) for i in range(nf)])


def exchange_bands(block, first):
    n = lax.axis_size("band")
    pairs = []
    for b in range(first, n - 1, 2):
        pairs += [(b, b + 1), (b + 1, b)]
    return lax.ppermute(block, "band", pairs)


def unit_rows(block):
    shaped = block.reshape(HEADS, HEAD_DIM, block.shape[-1])
    mean = jnp.mean(shaped * shaped, axis=1, keepdims=True)
    return (shaped * lax.rsqrt(mean + epsilon)).reshape(block.shape)


def norm_kernel(gain_ref, state_ref, normed_ref):
    x = state_ref[...].astype(F32)
    scale = lax.rsqrt(jnp.mean(x * x, axis=-1, keepdims=True) + epsilon)
    normed_ref[...] = (x * scale * gain_ref[...]).astype(BF)


def kernel(
    n_time, n_bands, total_levels,
    meta, scales, tally, *rest,
):
    slots, states = n_bands, 2 + n_time
    normed, rest = rest[0], rest[1:]
    mine, rest = rest[:slots], rest[slots:]
    other, rest = rest[:slots], rest[slots:]
    out_ref, weights, final, qs, ks, vs, mix = rest
    lon, width = out_ref.shape
    band, frame, shift, level = meta[0], meta[1], meta[2], meta[3]
    parity = lax.rem(frame, 2)
    r1 = width // n_bands
    r3 = 3 * r1

    bands = slot_bands(band, parity, n_bands)
    for group, which in ((mine, parity), (other, 1 - parity)):
        for b, ref in zip(bands, group):
            weights[which, pl.ds(pl.multiple_of(b * r3, 16), r3), :] = ref[:r3, :]
            final[which, pl.ds(pl.multiple_of(b * r1, 16), r1), :] = ref[r3:, :]

    nt = (((1,), (1,)), ((), ()))

    def proj(which, part, x):
        return lax.dot_general(
            weights[which, part * width : (part + 1) * width, :], x, nt, preferred_element_type=F32
        )

    own = normed[0]
    qs[0] = unit_rows(proj(0, 0, own)).astype(BF)
    for j in range(3):
        x = normed[j]
        ks[j] = unit_rows(proj(0, 1, x)).astype(BF)
        vs[j] = proj(0, 2, x).astype(BF)
    kcol = lax.broadcasted_iota(jnp.int32, (lon, lon), 0)
    qcol = lax.broadcasted_iota(jnp.int32, (lon, lon), 1)

    def window(col):
        c = col - shift
        c = jnp.where(c < 0, c + lon, c)
        w = jnp.zeros_like(c)
        for edge in range(WINDOW, lon, WINDOW):
            w = w + (c >= edge).astype(jnp.int32)
        return w

    same = window(kcol) == window(qcol)
    side = 1 - 2 * (band % 2)
    biases = []
    for j, off in enumerate((0, side, -side)):
        row = band + off
        exists = (row >= 0) & (row < n_bands)
        limit = jnp.where(exists, tally[jnp.clip(row, 0, n_bands - 1)], 0)
        seen = same & (kcol < limit)
        if j == 0:
            seen = seen | (kcol == qcol)
        biases.append(jnp.where(seen, 0.0, FAR).astype(F32))
    tn = (((0,), (0,)), ((), ()))
    for h in range(HEADS):
        lo = h * HEAD_DIM
        hi = lo + HEAD_DIM
        factor = scales[0, h] * (LOG2E / math.sqrt(HEAD_DIM))
        q = qs[0, lo:hi, :]
        x = [
            lax.dot_general(ks[j, lo:hi, :], q, tn, preferred_element_type=F32) * factor + biases[j]
            for j in range(3)
        ]
        top = jnp.max(jnp.maximum(jnp.maximum(x[0], x[1]), x[2]), axis=0, keepdims=True)
        e = [jnp.exp2(s - top) for s in x]
        inv = 1.0 / jnp.sum(e[0] + e[1] + e[2], axis=0, keepdims=True)
        o = sum(
            jnp.dot(vs[j, lo:hi, :], (e[j] * inv).astype(BF), preferred_element_type=F32)
            for j in range(3)
        )
        mix[0, lo:hi, :] = o.astype(BF)

    qs[1] = unit_rows(proj(1, 0, own)).astype(BF)
    for j in range(n_time):
        x = normed[j + 2 if j else 0]
        ks[3 + j] = unit_rows(proj(1, 1, x)).astype(BF)
        vs[3 + j] = proj(1, 2, x).astype(BF)
    odd = frame % 2
    back = [0, 2, jnp.where(odd == 1, 1, -1), jnp.where(odd == 1, 3, 1), jnp.where(odd == 1, -1, 3)]
    allow = [(b >= 0) & (b <= PRIOR_SNAPSHOTS) & (frame - b >= 0) for b in back]
    shut = [jnp.where(a, 0.0, FAR).astype(F32) for a in allow]
    for h in range(HEADS):
        lo = h * HEAD_DIM
        hi = lo + HEAD_DIM
        factor = scales[1, h] * (LOG2E / math.sqrt(HEAD_DIM))
        q = qs[1, lo:hi, :].astype(F32)
        x = [
            jnp.sum(q * ks[3 + j, lo:hi, :].astype(F32), axis=0, keepdims=True) * factor + shut[j]
            for j in range(n_time)
        ]
        top = functools.reduce(jnp.maximum, x)
        e = [jnp.exp2(s - top) for s in x]
        inv = 1.0 / sum(e)
        o = sum(
            (e[j] * inv).astype(BF).astype(F32) * vs[3 + j, lo:hi, :].astype(F32)
            for j in range(n_time)
        )
        mix[1, lo:hi, :] = o.astype(BF)

    update = jnp.dot(final[0], mix[0], preferred_element_type=F32) + jnp.dot(
        final[1], mix[1], preferred_element_type=F32
    )
    update = update.T

    def sigma_of(lv):
        power = (jnp.full((1, width), lv, jnp.int32).astype(F32) + 1.0) / total_levels
        return sigma_low * jnp.exp(power * math.log(sigma_high / sigma_low))

    s, s_next = sigma_of(level), sigma_of(level - 1)
    state = normed[states].astype(F32)
    fresh = normed[states + 1].astype(F32)
    denoised = state / (1.0 + s * s) + s * lax.rsqrt(1.0 + s * s) * update
    stepped = denoised + s_next * (keep_share * (state - denoised) / s + fresh_share * fresh)
    out_ref[...] = jnp.where(level == 0, sigma_high * fresh, stepped).astype(BF)


def body(
    noisy_snapshot_stack,
    gaussian_perturbation,
    snapshot_noise_indices,
    partition_longitude_starts,
    latitude_patch_tally,
    normalizer_scaling,
    head_score_scales,
    local_projection_matrices,
    time_projection_matrices,
    final_projection_matrices,
):
    frames, rows, lon, width = noisy_snapshot_stack.shape
    assert frames == 1 and rows == 1
    n, nf = lax.axis_size("band"), lax.axis_size("frame")
    assert n % 2 == 0 and nf % 2 == 0
    band, frame = lax.axis_index("band"), lax.axis_index("frame")
    parity = frame % 2
    state = noisy_snapshot_stack.reshape(lon, width)
    noise = gaussian_perturbation.reshape(lon, width)

    smem = pl.BlockSpec(memory_space=pltpu.SMEM)
    vmem = pl.BlockSpec(memory_space=pltpu.VMEM)
    hbm = pl.BlockSpec(memory_space=pltpu.HBM)
    gain = normalizer_scaling.reshape(1, width)
    normed = pl.pallas_call(
        norm_kernel,
        out_shape=jax.ShapeDtypeStruct((lon, width), BF),
        in_specs=[vmem, vmem],
        out_specs=vmem,
        compiler_params=pltpu.CompilerParams(vmem_limit_bytes=LARGE),
        name="norm",
    )(gain, state)

    chunk_a = jnp.concatenate([local_projection_matrices, final_projection_matrices[:width]], axis=1).T
    chunk_b = jnp.concatenate([time_projection_matrices, final_projection_matrices[width:]], axis=1).T
    own0 = jnp.where(parity == 0, chunk_a, chunk_b)
    own1 = jnp.where(parity == 0, chunk_b, chunk_a)

    meta = jnp.stack(
        [band, frame, partition_longitude_starts[0], snapshot_noise_indices[0]]
    ).astype(jnp.int32)
    ring, core = ring_pairs(nf, n), core_pairs(nf, n)
    half = n // 2
    chain0, chain1 = [own0], [own1]
    partners = exchange_bands(normed, 0)
    others = exchange_bands(normed, 1)
    two_back = rotate_frame(normed, 2)
    for h in range(half):
        a, b = chain0[-1], chain1[-1]
        if h == 1:
            a, meta = lax.optimization_barrier((a, meta))
        chain0.append(lax.ppermute(a, AXES, ring))
        if h < half - 1:
            chain1.append(lax.ppermute(b, AXES, ring))
    swap0 = [lax.ppermute(c, AXES, core) for c in chain0[1:half]]
    swap1 = [lax.ppermute(c, AXES, core) for c in chain1[1:half]]
    swap_last = lax.ppermute(chain0[half], AXES, core)
    mine = chain0 + swap1
    other = chain1 + [swap_last] + swap0
    partner = lax.ppermute(normed, AXES, core)
    partner_two = lax.ppermute(two_back, AXES, core)
    past = [two_back, partner, partner_two]
    if nf > 4:
        past.append(rotate_frame(normed, 3))

    n_time = 1 + len(past)
    rows_in = jnp.stack([normed, partners, others, *past, state, noise])
    out = pl.pallas_call(
        functools.partial(kernel, n_time, n, nf),
        out_shape=jax.ShapeDtypeStruct((lon, width), BF),
        in_specs=[smem] * 3 + [vmem] * (1 + 2 * n),
        out_specs=vmem,
        scratch_shapes=[
            pltpu.VMEM((2, 3 * width, width), BF),
            pltpu.VMEM((2, width, width), BF),
            pltpu.VMEM((2, width, lon), BF),
            pltpu.VMEM((3 + n_time, width, lon), BF),
            pltpu.VMEM((3 + n_time, width, lon), BF),
            pltpu.VMEM((2, width, lon), BF),
        ],
        compiler_params=pltpu.CompilerParams(vmem_limit_bytes=20 * 1024 * 1024),
        name="block",
    )(
        meta, head_score_scales, latitude_patch_tally,
        rows_in, *mine, *other,
    )
    return out.reshape(noisy_snapshot_stack.shape)


def solution(mesh):
    return jax.shard_map(
        body,
        mesh=mesh,
        in_specs=(
            P("frame", "band", None, None),
            P("frame", "band", None, None),
            P("frame"),
            P("frame"),
            P(),
            P(),
            P(),
            P(None, "band"),
            P(None, "band"),
            P(None, "band"),
        ),
        out_specs=P("frame", "band", None, None),
        check_vma=False,
    )
```

```python
import functools
import math

import jax
import jax.numpy as jnp
from jax import lax
from jax.experimental import pallas as pl
from jax.experimental.pallas import tpu as pltpu
from jax.sharding import PartitionSpec as P

HEADS = 8
HEAD_DIM = 64
WINDOW = 60
PRIOR_SNAPSHOTS = 3

epsilon = 1e-06
sigma_low = 0.1
sigma_high = 2.0
keep_share = 0.8
fresh_share = 0.6
LOG2E = 1.4426950408889634
FAR = -1e30
TIE = 9
LARGE = 60 * 1024 * 1024

AXES = ("frame", "band")
BF = jnp.bfloat16
F32 = jnp.float32


def slot_bands(band, parity, n):
    even = lax.rem(band, 2) == 0
    pos = jnp.where(even, band // 2, n - 1 - band // 2)
    half = n // 2
    bands = []
    for away in [*range(0, half + 1), *range(-1, -half, -1)]:
        p = lax.rem(pos + jnp.where(parity == 0, n - away, n + away), n)
        bands.append(jnp.where(p < half, 2 * p, 2 * (n - 1 - p) + 1))
    return bands


def ring_pairs(nf, n):
    order = list(range(0, n, 2)) + list(range(1, n, 2))[::-1]
    pairs = []
    for f in range(nf):
        step = 1 if f % 2 == 0 else -1
        for p in range(n):
            pairs.append((f * n + order[p], f * n + order[(p + step) % n]))
    return pairs


def core_pairs(nf, n, first=0, stride=1):
    return [(f * n + b, (f ^ 1) * n + b) for f in range(first, nf, stride) for b in range(n)]


def rotate_frame(block, hop):
    nf = lax.axis_size("frame")
    return lax.ppermute(block, "frame", [(i, (i + hop) % nf) for i in range(nf)])


def exchange_bands(block, first):
    n = lax.axis_size("band")
    pairs = []
    for b in range(first, n - 1, 2):
        pairs += [(b, b + 1), (b + 1, b)]
    return lax.ppermute(block, "band", pairs)


def unit_rows(block):
    shaped = block.reshape(HEADS, HEAD_DIM, block.shape[-1])
    mean = jnp.mean(shaped * shaped, axis=1, keepdims=True)
    return (shaped * lax.rsqrt(mean + epsilon)).reshape(block.shape)


def norm_kernel(gain_ref, rows_ref, normed_ref):
    for j in range(rows_ref.shape[0]):
        x = rows_ref[j].astype(F32)
        scale = lax.rsqrt(jnp.mean(x * x, axis=-1, keepdims=True) + epsilon)
        normed_ref[j] = (x * scale * gain_ref[...]).astype(BF)


def kernel(
    n_time, n_bands, total_levels,
    meta, scales, tally, *rest,
):
    slots, states = n_bands, 2 + n_time
    normed, late, rest = rest[0], rest[1], rest[2:]
    mine, rest = rest[:slots], rest[slots:]
    other, rest = rest[:slots], rest[slots:]
    out_ref, weights, final, qs, ks, vs, mix = rest
    lon, width = out_ref.shape
    band, frame, shift, level = meta[0], meta[1], meta[2], meta[3]
    parity = lax.rem(frame, 2)
    r1 = width // n_bands
    r3 = 3 * r1

    bands = slot_bands(band, parity, n_bands)
    for group, which in ((mine, parity), (other, 1 - parity)):
        for b, ref in zip(bands, group):
            weights[which, pl.ds(pl.multiple_of(b * r3, 16), r3), :] = ref[:r3, :]
            final[which, pl.ds(pl.multiple_of(b * r1, 16), r1), :] = ref[r3:, :]

    nt = (((1,), (1,)), ((), ()))

    def proj(which, part, x):
        return lax.dot_general(
            weights[which, part * width : (part + 1) * width, :], x, nt, preferred_element_type=F32
        )

    own = normed[0]
    qs[0] = unit_rows(proj(0, 0, own)).astype(BF)
    for j in range(3):
        x = normed[j]
        ks[j] = unit_rows(proj(0, 1, x)).astype(BF)
        vs[j] = proj(0, 2, x).astype(BF)
    kcol = lax.broadcasted_iota(jnp.int32, (lon, lon), 0)
    qcol = lax.broadcasted_iota(jnp.int32, (lon, lon), 1)

    def window(col):
        c = col - shift
        c = jnp.where(c < 0, c + lon, c)
        w = jnp.zeros_like(c)
        for edge in range(WINDOW, lon, WINDOW):
            w = w + (c >= edge).astype(jnp.int32)
        return w

    same = window(kcol) == window(qcol)
    side = 1 - 2 * (band % 2)
    biases = []
    for j, off in enumerate((0, side, -side)):
        row = band + off
        exists = (row >= 0) & (row < n_bands)
        limit = jnp.where(exists, tally[jnp.clip(row, 0, n_bands - 1)], 0)
        seen = same & (kcol < limit)
        if j == 0:
            seen = seen | (kcol == qcol)
        biases.append(jnp.where(seen, 0.0, FAR).astype(F32))
    tn = (((0,), (0,)), ((), ()))
    def time_part(i):
        j, part = i // 2, 1 + i % 2
        if j == n_time:
            qs[1] = unit_rows(proj(1, 0, normed[0])).astype(BF)
            return
        out = proj(1, part, normed[j + 2 if j else 0])
        if part == 1:
            ks[3 + j] = unit_rows(out).astype(BF)
        else:
            vs[3 + j] = out.astype(BF)

    todo = 2 * n_time + 1
    for h in range(HEADS):
        lo = h * HEAD_DIM
        hi = lo + HEAD_DIM
        factor = scales[0, h] * (LOG2E / math.sqrt(HEAD_DIM))
        q = qs[0, lo:hi, :]
        x = [
            lax.dot_general(ks[j, lo:hi, :], q, tn, preferred_element_type=F32) * factor + biases[j]
            for j in range(3)
        ]
        for i in range(h * todo // HEADS, (h + 1) * todo // HEADS):
            time_part(i)
        top = jnp.max(jnp.maximum(jnp.maximum(x[0], x[1]), x[2]), axis=0, keepdims=True)
        e = [jnp.exp2(s - top) for s in x]
        inv = 1.0 / jnp.sum(e[0] + e[1] + e[2], axis=0, keepdims=True)
        o = sum(
            jnp.dot(vs[j, lo:hi, :], e[j].astype(BF), preferred_element_type=F32)
            for j in range(3)
        )
        mix[0, lo:hi, :] = (o * inv).astype(BF)

    odd = frame % 2
    back = [0, 2, jnp.where(odd == 1, 1, -1), jnp.where(odd == 1, 3, 1), jnp.where(odd == 1, -1, 3)]
    allow = [(b >= 0) & (b <= PRIOR_SNAPSHOTS) & (frame - b >= 0) for b in back]
    shut = [jnp.where(a, 0.0, FAR).astype(F32) for a in allow]
    for h in range(HEADS):
        lo = h * HEAD_DIM
        hi = lo + HEAD_DIM
        factor = scales[1, h] * (LOG2E / math.sqrt(HEAD_DIM))
        q = qs[1, lo:hi, :].astype(F32)
        x = [
            jnp.sum(q * ks[3 + j, lo:hi, :].astype(F32), axis=0, keepdims=True) * factor + shut[j]
            for j in range(n_time)
        ]
        top = functools.reduce(jnp.maximum, x)
        e = [jnp.exp2(s - top) for s in x]
        inv = 1.0 / sum(e)
        o = sum(
            (e[j] * inv).astype(BF).astype(F32) * vs[3 + j, lo:hi, :].astype(F32)
            for j in range(n_time)
        )
        mix[1, lo:hi, :] = o.astype(BF)

    update = jnp.dot(final[0], mix[0], preferred_element_type=F32) + jnp.dot(
        final[1], mix[1], preferred_element_type=F32
    )
    update = update.T

    def sigma_of(lv):
        power = (jnp.full((1, width), lv, jnp.int32).astype(F32) + 1.0) / total_levels
        return sigma_low * jnp.exp(power * math.log(sigma_high / sigma_low))

    s, s_next = sigma_of(level), sigma_of(level - 1)
    state = late[0].astype(F32)
    fresh = late[1].astype(F32)
    denoised = state / (1.0 + s * s) + s * lax.rsqrt(1.0 + s * s) * update
    stepped = denoised + s_next * (keep_share * (state - denoised) / s + fresh_share * fresh)
    out_ref[...] = jnp.where(level == 0, sigma_high * fresh, stepped).astype(BF)


def body(
    noisy_snapshot_stack,
    gaussian_perturbation,
    snapshot_noise_indices,
    partition_longitude_starts,
    latitude_patch_tally,
    normalizer_scaling,
    head_score_scales,
    local_projection_matrices,
    time_projection_matrices,
    final_projection_matrices,
):
    frames, rows, lon, width = noisy_snapshot_stack.shape
    assert frames == 1 and rows == 1
    n, nf = lax.axis_size("band"), lax.axis_size("frame")
    assert n % 2 == 0 and nf % 2 == 0
    band, frame = lax.axis_index("band"), lax.axis_index("frame")
    parity = frame % 2
    state = noisy_snapshot_stack.reshape(lon, width)
    noise = gaussian_perturbation.reshape(lon, width)

    smem = pl.BlockSpec(memory_space=pltpu.SMEM)
    vmem = pl.BlockSpec(memory_space=pltpu.VMEM)
    hbm = pl.BlockSpec(memory_space=pltpu.HBM)
    chunk_a = jnp.concatenate([local_projection_matrices, final_projection_matrices[:width]], axis=1).T
    chunk_b = jnp.concatenate([time_projection_matrices, final_projection_matrices[width:]], axis=1).T
    own0 = jnp.where(parity == 0, chunk_a, chunk_b)
    own1 = jnp.where(parity == 0, chunk_b, chunk_a)

    meta = jnp.stack(
        [band, frame, partition_longitude_starts[0], snapshot_noise_indices[0]]
    ).astype(jnp.int32)
    ring, core = ring_pairs(nf, n), core_pairs(nf, n)
    half = n // 2
    chain0, chain1 = [own0], [own1]
    partners = exchange_bands(state, 0)
    others = exchange_bands(state, 1)
    two_back = rotate_frame(state, 2)
    for h in range(half):
        a, b = chain0[-1], chain1[-1]
        if h == 1:
            a, meta = lax.optimization_barrier((a, meta))
        chain0.append(lax.ppermute(a, AXES, ring))
        if h < half - 1:
            chain1.append(lax.ppermute(b, AXES, ring))
    swap0 = [lax.ppermute(c, AXES, core) for c in chain0[1:half]]
    swap1 = [lax.ppermute(c, AXES, core) for c in chain1[1:half]]
    swap_last = lax.ppermute(chain0[half], AXES, core)
    mine = chain0 + swap1
    other = chain1 + [swap_last] + swap0
    partner = lax.ppermute(state, AXES, core)
    partner_two = lax.ppermute(two_back, AXES, core)
    past = [two_back, partner, partner_two]
    if nf > 4:
        past.append(rotate_frame(state, 3))

    n_time = 1 + len(past)
    gathered = jnp.stack([state, partners, others, *past])
    normed = pl.pallas_call(
        norm_kernel,
        out_shape=jax.ShapeDtypeStruct(gathered.shape, BF),
        in_specs=[vmem, vmem],
        out_specs=vmem,
        compiler_params=pltpu.CompilerParams(vmem_limit_bytes=8 * 1024 * 1024),
        name="norm",
    )(normalizer_scaling.reshape(1, width), gathered)
    late = jnp.stack([state, noise])
    out = pl.pallas_call(
        functools.partial(kernel, n_time, n, nf),
        out_shape=jax.ShapeDtypeStruct((lon, width), BF),
        in_specs=[smem] * 3 + [vmem] * (2 + 2 * n),
        out_specs=vmem,
        scratch_shapes=[
            pltpu.VMEM((2, 3 * width, width), BF),
            pltpu.VMEM((2, width, width), BF),
            pltpu.VMEM((2, width, lon), BF),
            pltpu.VMEM((3 + n_time, width, lon), BF),
            pltpu.VMEM((3 + n_time, width, lon), BF),
            pltpu.VMEM((2, width, lon), BF),
        ],
        compiler_params=pltpu.CompilerParams(vmem_limit_bytes=20 * 1024 * 1024),
        name="block",
    )(
        meta, head_score_scales, latitude_patch_tally,
        normed, late, *mine, *other,
    )
    return out.reshape(noisy_snapshot_stack.shape)


def solution(mesh):
    return jax.shard_map(
        body,
        mesh=mesh,
        in_specs=(
            P("frame", "band", None, None),
            P("frame", "band", None, None),
            P("frame"),
            P("frame"),
            P(),
            P(),
            P(),
            P(None, "band"),
            P(None, "band"),
            P(None, "band"),
        ),
        out_specs=P("frame", "band", None, None),
        check_vma=False,
    )
```

```python
import functools
import math

import jax
import jax.numpy as jnp
from jax import lax
from jax.experimental import pallas as pl
from jax.experimental.pallas import tpu as pltpu
from jax.sharding import PartitionSpec as P

HEADS = 8
HEAD_DIM = 64
WINDOW = 60
PRIOR_SNAPSHOTS = 3

epsilon = 1e-06
sigma_low = 0.1
sigma_high = 2.0
keep_share = 0.8
fresh_share = 0.6
LOG2E = 1.4426950408889634
FAR = -1e30
TIE = 9
LARGE = 60 * 1024 * 1024

AXES = ("frame", "band")
BF = jnp.bfloat16
F32 = jnp.float32


def slot_bands(band, parity, n):
    even = lax.rem(band, 2) == 0
    pos = jnp.where(even, band // 2, n - 1 - band // 2)
    half = n // 2
    bands = []
    for away in [*range(0, half + 1), *range(-1, -half, -1)]:
        p = lax.rem(pos + jnp.where(parity == 0, n - away, n + away), n)
        bands.append(jnp.where(p < half, 2 * p, 2 * (n - 1 - p) + 1))
    return bands


def ring_pairs(nf, n):
    order = list(range(0, n, 2)) + list(range(1, n, 2))[::-1]
    pairs = []
    for f in range(nf):
        step = 1 if f % 2 == 0 else -1
        for p in range(n):
            pairs.append((f * n + order[p], f * n + order[(p + step) % n]))
    return pairs


def core_pairs(nf, n, first=0, stride=1):
    return [(f * n + b, (f ^ 1) * n + b) for f in range(first, nf, stride) for b in range(n)]


def rotate_frame(block, hop):
    nf = lax.axis_size("frame")
    return lax.ppermute(block, "frame", [(i, (i + hop) % nf) for i in range(nf)])


def exchange_bands(block, first):
    n = lax.axis_size("band")
    pairs = []
    for b in range(first, n - 1, 2):
        pairs += [(b, b + 1), (b + 1, b)]
    return lax.ppermute(block, "band", pairs)


def unit_rows(block):
    shaped = block.reshape(HEADS, HEAD_DIM, block.shape[-1])
    mean = jnp.mean(shaped * shaped, axis=1, keepdims=True)
    return (shaped * lax.rsqrt(mean + epsilon)).reshape(block.shape)


def norm_kernel(gain_ref, rows_ref, normed_ref):
    for j in range(rows_ref.shape[0]):
        x = rows_ref[j].astype(F32)
        scale = lax.rsqrt(jnp.mean(x * x, axis=-1, keepdims=True) + epsilon)
        normed_ref[j] = (x * scale * gain_ref[...]).astype(BF)


def kernel(
    n_time, n_bands, total_levels,
    meta, scales, tally, *rest,
):
    slots, states = n_bands, 2 + n_time
    normed, late, rest = rest[0], rest[1], rest[2:]
    mine, rest = rest[:slots], rest[slots:]
    other, rest = rest[:slots], rest[slots:]
    out_ref, weights, final, qs, ks, vs, mix = rest
    lon, width = out_ref.shape
    band, frame, shift, level = meta[0], meta[1], meta[2], meta[3]
    parity = lax.rem(frame, 2)
    r1 = width // n_bands
    r3 = 3 * r1

    bands = slot_bands(band, parity, n_bands)
    for group, which in ((mine, parity), (other, 1 - parity)):
        for b, ref in zip(bands, group):
            weights[which, pl.ds(pl.multiple_of(b * r3, 16), r3), :] = ref[:r3, :]
            final[which, pl.ds(pl.multiple_of(b * r1, 16), r1), :] = ref[r3:, :]

    nt = (((1,), (1,)), ((), ()))

    def proj(which, part, x):
        return lax.dot_general(
            weights[which, part * width : (part + 1) * width, :], x, nt, preferred_element_type=F32
        )

    own = normed[0]
    qs[0] = unit_rows(proj(0, 0, own)).astype(BF)
    for j in range(3):
        x = normed[j]
        ks[j] = unit_rows(proj(0, 1, x)).astype(BF)
        vs[j] = proj(0, 2, x).astype(BF)
    kcol = lax.broadcasted_iota(jnp.int32, (lon, lon), 0)
    qcol = lax.broadcasted_iota(jnp.int32, (lon, lon), 1)

    def window(col):
        c = col - shift
        c = jnp.where(c < 0, c + lon, c)
        w = jnp.zeros_like(c)
        for edge in range(WINDOW, lon, WINDOW):
            w = w + (c >= edge).astype(jnp.int32)
        return w

    same = window(kcol) == window(qcol)
    side = 1 - 2 * (band % 2)
    biases = []
    for j, off in enumerate((0, side, -side)):
        row = band + off
        exists = (row >= 0) & (row < n_bands)
        limit = jnp.where(exists, tally[jnp.clip(row, 0, n_bands - 1)], 0)
        seen = same & (kcol < limit)
        if j == 0:
            seen = seen | (kcol == qcol)
        biases.append(jnp.where(seen, 0.0, FAR).astype(F32))
    tn = (((0,), (0,)), ((), ()))
    def time_part(i):
        j, part = i // 2, 1 + i % 2
        if j == n_time:
            qs[1] = unit_rows(proj(1, 0, normed[0])).astype(BF)
            return
        out = proj(1, part, normed[j + 2 if j else 0])
        if part == 1:
            ks[3 + j] = unit_rows(out).astype(BF)
        else:
            vs[3 + j] = out.astype(BF)

    todo = 2 * n_time + 1
    pairs = HEADS // 2
    wide = [jnp.concatenate([b, b], axis=1) for b in biases]
    first_half = lax.broadcasted_iota(jnp.int32, (1, 2 * lon), 1) < lon
    blank = jnp.zeros((HEAD_DIM, lon), BF)
    for h in range(pairs):
        lo = 2 * h * HEAD_DIM
        mid = lo + HEAD_DIM
        hi = mid + HEAD_DIM
        base = LOG2E / math.sqrt(HEAD_DIM)
        factor = jnp.where(first_half, scales[0, 2 * h] * base, scales[0, 2 * h + 1] * base)
        q = jnp.concatenate(
            [
                jnp.concatenate([qs[0, lo:mid, :], blank], axis=1),
                jnp.concatenate([blank, qs[0, mid:hi, :]], axis=1),
            ],
            axis=0,
        )
        x = [
            lax.dot_general(ks[j, lo:hi, :], q, tn, preferred_element_type=F32) * factor + wide[j]
            for j in range(3)
        ]
        for i in range(h * todo // pairs, (h + 1) * todo // pairs):
            time_part(i)
        top = jnp.max(jnp.maximum(jnp.maximum(x[0], x[1]), x[2]), axis=0, keepdims=True)
        e = [jnp.exp2(s - top) for s in x]
        inv = 1.0 / jnp.sum(e[0] + e[1] + e[2], axis=0, keepdims=True)
        o = sum(
            jnp.dot(vs[j, lo:hi, :], e[j].astype(BF), preferred_element_type=F32)
            for j in range(3)
        )
        o = o * inv
        mix[0, lo:mid, :] = o[:HEAD_DIM, :lon].astype(BF)
        mix[0, mid:hi, :] = o[HEAD_DIM:, lon:].astype(BF)

    odd = frame % 2
    back = [0, 2, jnp.where(odd == 1, 1, -1), jnp.where(odd == 1, 3, 1), jnp.where(odd == 1, -1, 3)]
    allow = [(b >= 0) & (b <= PRIOR_SNAPSHOTS) & (frame - b >= 0) for b in back]
    shut = [jnp.where(a, 0.0, FAR).astype(F32) for a in allow]
    for h in range(HEADS):
        lo = h * HEAD_DIM
        hi = lo + HEAD_DIM
        factor = scales[1, h] * (LOG2E / math.sqrt(HEAD_DIM))
        q = qs[1, lo:hi, :].astype(F32)
        x = [
            jnp.sum(q * ks[3 + j, lo:hi, :].astype(F32), axis=0, keepdims=True) * factor + shut[j]
            for j in range(n_time)
        ]
        top = functools.reduce(jnp.maximum, x)
        e = [jnp.exp2(s - top) for s in x]
        inv = 1.0 / sum(e)
        o = sum(
            (e[j] * inv).astype(BF).astype(F32) * vs[3 + j, lo:hi, :].astype(F32)
            for j in range(n_time)
        )
        mix[1, lo:hi, :] = o.astype(BF)

    update = jnp.dot(final[0], mix[0], preferred_element_type=F32) + jnp.dot(
        final[1], mix[1], preferred_element_type=F32
    )
    update = update.T

    def sigma_of(lv):
        power = (jnp.full((1, width), lv, jnp.int32).astype(F32) + 1.0) / total_levels
        return sigma_low * jnp.exp(power * math.log(sigma_high / sigma_low))

    s, s_next = sigma_of(level), sigma_of(level - 1)
    state = late[0].astype(F32)
    fresh = late[1].astype(F32)
    denoised = state / (1.0 + s * s) + s * lax.rsqrt(1.0 + s * s) * update
    stepped = denoised + s_next * (keep_share * (state - denoised) / s + fresh_share * fresh)
    out_ref[...] = jnp.where(level == 0, sigma_high * fresh, stepped).astype(BF)


def body(
    noisy_snapshot_stack,
    gaussian_perturbation,
    snapshot_noise_indices,
    partition_longitude_starts,
    latitude_patch_tally,
    normalizer_scaling,
    head_score_scales,
    local_projection_matrices,
    time_projection_matrices,
    final_projection_matrices,
):
    frames, rows, lon, width = noisy_snapshot_stack.shape
    assert frames == 1 and rows == 1
    n, nf = lax.axis_size("band"), lax.axis_size("frame")
    assert n % 2 == 0 and nf % 2 == 0
    band, frame = lax.axis_index("band"), lax.axis_index("frame")
    parity = frame % 2
    state = noisy_snapshot_stack.reshape(lon, width)
    noise = gaussian_perturbation.reshape(lon, width)

    smem = pl.BlockSpec(memory_space=pltpu.SMEM)
    vmem = pl.BlockSpec(memory_space=pltpu.VMEM)
    hbm = pl.BlockSpec(memory_space=pltpu.HBM)
    chunk_a = jnp.concatenate([local_projection_matrices, final_projection_matrices[:width]], axis=1).T
    chunk_b = jnp.concatenate([time_projection_matrices, final_projection_matrices[width:]], axis=1).T
    own0 = jnp.where(parity == 0, chunk_a, chunk_b)
    own1 = jnp.where(parity == 0, chunk_b, chunk_a)

    meta = jnp.stack(
        [band, frame, partition_longitude_starts[0], snapshot_noise_indices[0]]
    ).astype(jnp.int32)
    ring, core = ring_pairs(nf, n), core_pairs(nf, n)
    half = n // 2
    chain0, chain1 = [own0], [own1]
    partners = exchange_bands(state, 0)
    others = exchange_bands(state, 1)
    two_back = rotate_frame(state, 2)
    for h in range(half):
        a, b = chain0[-1], chain1[-1]
        if h == 1:
            a, meta = lax.optimization_barrier((a, meta))
        chain0.append(lax.ppermute(a, AXES, ring))
        if h < half - 1:
            chain1.append(lax.ppermute(b, AXES, ring))
    swap0 = [lax.ppermute(c, AXES, core) for c in chain0[1:half]]
    swap1 = [lax.ppermute(c, AXES, core) for c in chain1[1:half]]
    swap_last = lax.ppermute(chain0[half], AXES, core)
    mine = chain0 + swap1
    other = chain1 + [swap_last] + swap0
    partner = lax.ppermute(state, AXES, core)
    partner_two = lax.ppermute(two_back, AXES, core)
    past = [two_back, partner, partner_two]
    if nf > 4:
        past.append(rotate_frame(state, 3))

    n_time = 1 + len(past)
    gathered = jnp.stack([state, partners, others, *past])
    normed = pl.pallas_call(
        norm_kernel,
        out_shape=jax.ShapeDtypeStruct(gathered.shape, BF),
        in_specs=[vmem, vmem],
        out_specs=vmem,
        compiler_params=pltpu.CompilerParams(vmem_limit_bytes=8 * 1024 * 1024),
        name="norm",
    )(normalizer_scaling.reshape(1, width), gathered)
    late = jnp.stack([state, noise])
    out = pl.pallas_call(
        functools.partial(kernel, n_time, n, nf),
        out_shape=jax.ShapeDtypeStruct((lon, width), BF),
        in_specs=[smem] * 3 + [vmem] * (2 + 2 * n),
        out_specs=vmem,
        scratch_shapes=[
            pltpu.VMEM((2, 3 * width, width), BF),
            pltpu.VMEM((2, width, width), BF),
            pltpu.VMEM((2, width, lon), BF),
            pltpu.VMEM((3 + n_time, width, lon), BF),
            pltpu.VMEM((3 + n_time, width, lon), BF),
            pltpu.VMEM((2, width, lon), BF),
        ],
        compiler_params=pltpu.CompilerParams(vmem_limit_bytes=20 * 1024 * 1024),
        name="block",
    )(
        meta, head_score_scales, latitude_patch_tally,
        normed, late, *mine, *other,
    )
    return out.reshape(noisy_snapshot_stack.shape)


def solution(mesh):
    return jax.shard_map(
        body,
        mesh=mesh,
        in_specs=(
            P("frame", "band", None, None),
            P("frame", "band", None, None),
            P("frame"),
            P("frame"),
            P(),
            P(),
            P(),
            P(None, "band"),
            P(None, "band"),
            P(None, "band"),
        ),
        out_specs=P("frame", "band", None, None),
        check_vma=False,
    )
```

```python
import functools
import math

import jax
import jax.numpy as jnp
from jax import lax
from jax.experimental import pallas as pl
from jax.experimental.pallas import tpu as pltpu
from jax.sharding import PartitionSpec as P

HEADS = 8
HEAD_DIM = 64
WINDOW = 60
PRIOR_SNAPSHOTS = 3

epsilon = 1e-06
sigma_low = 0.1
sigma_high = 2.0
keep_share = 0.8
fresh_share = 0.6
LOG2E = 1.4426950408889634
FAR = -1e30
TIE = 9
LARGE = 60 * 1024 * 1024

AXES = ("frame", "band")
BF = jnp.bfloat16
F32 = jnp.float32


def slot_bands(band, parity, n):
    even = lax.rem(band, 2) == 0
    pos = jnp.where(even, band // 2, n - 1 - band // 2)
    half = n // 2
    bands = []
    for away in [*range(0, half + 1), *range(-1, -half, -1)]:
        p = lax.rem(pos + jnp.where(parity == 0, n - away, n + away), n)
        bands.append(jnp.where(p < half, 2 * p, 2 * (n - 1 - p) + 1))
    return bands


def ring_pairs(nf, n):
    order = list(range(0, n, 2)) + list(range(1, n, 2))[::-1]
    pairs = []
    for f in range(nf):
        step = 1 if f % 2 == 0 else -1
        for p in range(n):
            pairs.append((f * n + order[p], f * n + order[(p + step) % n]))
    return pairs


def core_pairs(nf, n, first=0, stride=1):
    return [(f * n + b, (f ^ 1) * n + b) for f in range(first, nf, stride) for b in range(n)]


def rotate_frame(block, hop):
    nf = lax.axis_size("frame")
    return lax.ppermute(block, "frame", [(i, (i + hop) % nf) for i in range(nf)])


def exchange_bands(block, first):
    n = lax.axis_size("band")
    pairs = []
    for b in range(first, n - 1, 2):
        pairs += [(b, b + 1), (b + 1, b)]
    return lax.ppermute(block, "band", pairs)


def unit_rows(block):
    shaped = block.reshape(HEADS, HEAD_DIM, block.shape[-1])
    mean = jnp.mean(shaped * shaped, axis=1, keepdims=True)
    return (shaped * lax.rsqrt(mean + epsilon)).reshape(block.shape)


def norm_kernel(gain_ref, rows_ref, normed_ref):
    for j in range(rows_ref.shape[0]):
        x = rows_ref[j].astype(F32)
        scale = lax.rsqrt(jnp.mean(x * x, axis=-1, keepdims=True) + epsilon)
        normed_ref[j] = (x * scale * gain_ref[...]).astype(BF)


def kernel(
    n_time, n_bands, total_levels,
    meta, scales, tally, *rest,
):
    slots, states = n_bands, 2 + n_time
    normed, late, rest = rest[0], rest[1], rest[2:]
    mine, rest = rest[:slots], rest[slots:]
    other, rest = rest[:slots], rest[slots:]
    out_ref, weights, final, qs, ks, vs, mix = rest
    lon, width = out_ref.shape
    band, frame, shift, level = meta[0], meta[1], meta[2], meta[3]
    parity = lax.rem(frame, 2)
    r1 = width // n_bands
    r3 = 3 * r1

    bands = slot_bands(band, parity, n_bands)
    for group, which in ((mine, parity), (other, 1 - parity)):
        for b, ref in zip(bands, group):
            weights[which, pl.ds(pl.multiple_of(b * r3, 16), r3), :] = ref[:r3, :]
            final[which, pl.ds(pl.multiple_of(b * r1, 16), r1), :] = ref[r3:, :]

    nt = (((1,), (1,)), ((), ()))

    def proj(which, part, x):
        return lax.dot_general(
            weights[which, part * width : (part + 1) * width, :], x, nt, preferred_element_type=F32
        )

    own = normed[0]
    qs[0] = unit_rows(proj(0, 0, own)).astype(BF)
    for j in range(3):
        x = normed[j]
        ks[j] = unit_rows(proj(0, 1, x)).astype(BF)
        vs[j] = proj(0, 2, x).astype(BF)
    kcol = lax.broadcasted_iota(jnp.int32, (lon, 1), 0)
    qcol = lax.broadcasted_iota(jnp.int32, (1, lon), 1)

    def window(col):
        c = col - shift
        c = jnp.where(c < 0, c + lon, c)
        w = jnp.zeros_like(c)
        for edge in range(WINDOW, lon, WINDOW):
            w = w + (c >= edge).astype(jnp.int32)
        return w

    same = window(kcol) == window(qcol)
    side = 1 - 2 * (band % 2)
    biases = []
    for j, off in enumerate((0, side, -side)):
        row = band + off
        exists = (row >= 0) & (row < n_bands)
        limit = jnp.where(exists, tally[jnp.clip(row, 0, n_bands - 1)], 0)
        seen = same & (kcol < limit)
        if j == 0:
            seen = seen | (kcol == qcol)
        biases.append(jnp.where(seen, 0.0, FAR).astype(F32))
    tn = (((0,), (0,)), ((), ()))
    def time_part(i):
        j, part = i // 2, 1 + i % 2
        if j == n_time:
            qs[1] = unit_rows(proj(1, 0, normed[0])).astype(BF)
            return
        out = proj(1, part, normed[j + 2 if j else 0])
        if part == 1:
            ks[3 + j] = unit_rows(out).astype(BF)
        else:
            vs[3 + j] = out.astype(BF)

    todo = 2 * n_time + 1
    pairs = HEADS // 2
    wide = [jnp.concatenate([b, b], axis=1) for b in biases]
    first_half = lax.broadcasted_iota(jnp.int32, (1, 2 * lon), 1) < lon
    blank = jnp.zeros((HEAD_DIM, lon), BF)
    for h in range(pairs):
        lo = 2 * h * HEAD_DIM
        mid = lo + HEAD_DIM
        hi = mid + HEAD_DIM
        base = LOG2E / math.sqrt(HEAD_DIM)
        factor = jnp.where(first_half, scales[0, 2 * h] * base, scales[0, 2 * h + 1] * base)
        q = jnp.concatenate(
            [
                jnp.concatenate([qs[0, lo:mid, :], blank], axis=1),
                jnp.concatenate([blank, qs[0, mid:hi, :]], axis=1),
            ],
            axis=0,
        )
        x = [
            lax.dot_general(ks[j, lo:hi, :], q, tn, preferred_element_type=F32) * factor + wide[j]
            for j in range(3)
        ]
        for i in range(h * todo // pairs, (h + 1) * todo // pairs):
            time_part(i)
        top = jnp.max(jnp.maximum(jnp.maximum(x[0], x[1]), x[2]), axis=0, keepdims=True)
        e = [jnp.exp2(s - top) for s in x]
        inv = 1.0 / jnp.sum(e[0] + e[1] + e[2], axis=0, keepdims=True)
        o = sum(
            jnp.dot(vs[j, lo:hi, :], e[j].astype(BF), preferred_element_type=F32)
            for j in range(3)
        )
        o = o * inv
        mix[0, lo:mid, :] = o[:HEAD_DIM, :lon].astype(BF)
        mix[0, mid:hi, :] = o[HEAD_DIM:, lon:].astype(BF)

    odd = frame % 2
    back = [0, 2, jnp.where(odd == 1, 1, -1), jnp.where(odd == 1, 3, 1), jnp.where(odd == 1, -1, 3)]
    allow = [(b >= 0) & (b <= PRIOR_SNAPSHOTS) & (frame - b >= 0) for b in back]
    shut = [jnp.where(a, 0.0, FAR).astype(F32) for a in allow]
    for h in range(HEADS):
        lo = h * HEAD_DIM
        hi = lo + HEAD_DIM
        factor = scales[1, h] * (LOG2E / math.sqrt(HEAD_DIM))
        q = qs[1, lo:hi, :].astype(F32)
        x = [
            jnp.sum(q * ks[3 + j, lo:hi, :].astype(F32), axis=0, keepdims=True) * factor + shut[j]
            for j in range(n_time)
        ]
        top = functools.reduce(jnp.maximum, x)
        e = [jnp.exp2(s - top) for s in x]
        inv = 1.0 / sum(e)
        o = sum(
            (e[j] * inv).astype(BF).astype(F32) * vs[3 + j, lo:hi, :].astype(F32)
            for j in range(n_time)
        )
        mix[1, lo:hi, :] = o.astype(BF)

    update = sum(
        lax.dot_general(mix[w], final[w], (((0,), (1,)), ((), ())), preferred_element_type=F32)
        for w in (0, 1)
    )

    def sigma_of(lv):
        power = (jnp.full((1, width), lv, jnp.int32).astype(F32) + 1.0) / total_levels
        return sigma_low * jnp.exp(power * math.log(sigma_high / sigma_low))

    s, s_next = sigma_of(level), sigma_of(level - 1)
    state = late[0].astype(F32)
    fresh = late[1].astype(F32)
    denoised = state / (1.0 + s * s) + s * lax.rsqrt(1.0 + s * s) * update
    stepped = denoised + s_next * (keep_share * (state - denoised) / s + fresh_share * fresh)
    out_ref[...] = jnp.where(level == 0, sigma_high * fresh, stepped).astype(BF)


def body(
    noisy_snapshot_stack,
    gaussian_perturbation,
    snapshot_noise_indices,
    partition_longitude_starts,
    latitude_patch_tally,
    normalizer_scaling,
    head_score_scales,
    local_projection_matrices,
    time_projection_matrices,
    final_projection_matrices,
):
    frames, rows, lon, width = noisy_snapshot_stack.shape
    assert frames == 1 and rows == 1
    n, nf = lax.axis_size("band"), lax.axis_size("frame")
    assert n % 2 == 0 and nf % 2 == 0
    band, frame = lax.axis_index("band"), lax.axis_index("frame")
    parity = frame % 2
    state = noisy_snapshot_stack.reshape(lon, width)
    noise = gaussian_perturbation.reshape(lon, width)

    smem = pl.BlockSpec(memory_space=pltpu.SMEM)
    vmem = pl.BlockSpec(memory_space=pltpu.VMEM)
    hbm = pl.BlockSpec(memory_space=pltpu.HBM)
    chunk_a = jnp.concatenate([local_projection_matrices, final_projection_matrices[:width]], axis=1).T
    chunk_b = jnp.concatenate([time_projection_matrices, final_projection_matrices[width:]], axis=1).T
    own0 = jnp.where(parity == 0, chunk_a, chunk_b)
    own1 = jnp.where(parity == 0, chunk_b, chunk_a)

    meta = jnp.stack(
        [band, frame, partition_longitude_starts[0], snapshot_noise_indices[0]]
    ).astype(jnp.int32)
    ring, core = ring_pairs(nf, n), core_pairs(nf, n)
    half = n // 2
    chain0, chain1 = [own0], [own1]
    partners = exchange_bands(state, 0)
    others = exchange_bands(state, 1)
    two_back = rotate_frame(state, 2)
    for h in range(half):
        a, b = chain0[-1], chain1[-1]
        if h == 1:
            a, meta = lax.optimization_barrier((a, meta))
        chain0.append(lax.ppermute(a, AXES, ring))
        if h < half - 1:
            chain1.append(lax.ppermute(b, AXES, ring))
    swap0 = [lax.ppermute(c, AXES, core) for c in chain0[1:half]]
    swap1 = [lax.ppermute(c, AXES, core) for c in chain1[1:half]]
    swap_last = lax.ppermute(chain0[half], AXES, core)
    mine = chain0 + swap1
    other = chain1 + [swap_last] + swap0
    partner = lax.ppermute(state, AXES, core)
    partner_two = lax.ppermute(two_back, AXES, core)
    past = [two_back, partner, partner_two]
    if nf > 4:
        past.append(rotate_frame(state, 3))

    n_time = 1 + len(past)
    gathered = jnp.stack([state, partners, others, *past])
    normed = pl.pallas_call(
        norm_kernel,
        out_shape=jax.ShapeDtypeStruct(gathered.shape, BF),
        in_specs=[vmem, vmem],
        out_specs=vmem,
        compiler_params=pltpu.CompilerParams(vmem_limit_bytes=8 * 1024 * 1024),
        name="norm",
    )(normalizer_scaling.reshape(1, width), gathered)
    late = jnp.stack([state, noise])
    out = pl.pallas_call(
        functools.partial(kernel, n_time, n, nf),
        out_shape=jax.ShapeDtypeStruct((lon, width), BF),
        in_specs=[smem] * 3 + [vmem] * (2 + 2 * n),
        out_specs=vmem,
        scratch_shapes=[
            pltpu.VMEM((2, 3 * width, width), BF),
            pltpu.VMEM((2, width, width), BF),
            pltpu.VMEM((2, width, lon), BF),
            pltpu.VMEM((3 + n_time, width, lon), BF),
            pltpu.VMEM((3 + n_time, width, lon), BF),
            pltpu.VMEM((2, width, lon), BF),
        ],
        compiler_params=pltpu.CompilerParams(vmem_limit_bytes=20 * 1024 * 1024),
        name="block",
    )(
        meta, head_score_scales, latitude_patch_tally,
        normed, late, *mine, *other,
    )
    return out.reshape(noisy_snapshot_stack.shape)


def solution(mesh):
    return jax.shard_map(
        body,
        mesh=mesh,
        in_specs=(
            P("frame", "band", None, None),
            P("frame", "band", None, None),
            P("frame"),
            P("frame"),
            P(),
            P(),
            P(),
            P(None, "band"),
            P(None, "band"),
            P(None, "band"),
        ),
        out_specs=P("frame", "band", None, None),
        check_vma=False,
    )
```

```python
import functools
import math

import jax
import jax.numpy as jnp
from jax import lax
from jax.experimental import pallas as pl
from jax.experimental.pallas import tpu as pltpu
from jax.sharding import PartitionSpec as P

HEADS = 8
HEAD_DIM = 64
WINDOW = 60
PRIOR_SNAPSHOTS = 3

epsilon = 1e-06
sigma_low = 0.1
sigma_high = 2.0
keep_share = 0.8
fresh_share = 0.6
LOG2E = 1.4426950408889634
FAR = -1e30
TIE = 9
LARGE = 60 * 1024 * 1024

AXES = ("frame", "band")
BF = jnp.bfloat16
F32 = jnp.float32


def slot_bands(band, parity, n):
    even = lax.rem(band, 2) == 0
    pos = jnp.where(even, band // 2, n - 1 - band // 2)
    half = n // 2
    bands = []
    for away in [*range(0, half + 1), *range(-1, -half, -1)]:
        p = lax.rem(pos + jnp.where(parity == 0, n - away, n + away), n)
        bands.append(jnp.where(p < half, 2 * p, 2 * (n - 1 - p) + 1))
    return bands


def ring_pairs(nf, n):
    order = list(range(0, n, 2)) + list(range(1, n, 2))[::-1]
    pairs = []
    for f in range(nf):
        step = 1 if f % 2 == 0 else -1
        for p in range(n):
            pairs.append((f * n + order[p], f * n + order[(p + step) % n]))
    return pairs


def core_pairs(nf, n, first=0, stride=1):
    return [(f * n + b, (f ^ 1) * n + b) for f in range(first, nf, stride) for b in range(n)]


def rotate_frame(block, hop):
    nf = lax.axis_size("frame")
    return lax.ppermute(block, "frame", [(i, (i + hop) % nf) for i in range(nf)])


def exchange_bands(block, first):
    n = lax.axis_size("band")
    pairs = []
    for b in range(first, n - 1, 2):
        pairs += [(b, b + 1), (b + 1, b)]
    return lax.ppermute(block, "band", pairs)


def unit_rows(block):
    shaped = block.reshape(HEADS, HEAD_DIM, block.shape[-1])
    mean = jnp.mean(shaped * shaped, axis=1, keepdims=True)
    return (shaped * lax.rsqrt(mean + epsilon)).reshape(block.shape)


def norm_kernel(gain_ref, rows_ref, normed_ref):
    for j in range(rows_ref.shape[0]):
        x = rows_ref[j].astype(F32)
        scale = lax.rsqrt(jnp.mean(x * x, axis=-1, keepdims=True) + epsilon)
        normed_ref[j] = (x * scale * gain_ref[...]).astype(BF)


def kernel(
    n_time, n_bands, total_levels,
    meta, scales, tally, *rest,
):
    slots, states = n_bands, 2 + n_time
    normed, late, rest = rest[0], rest[1], rest[2:]
    mine, rest = rest[:slots], rest[slots:]
    other, rest = rest[:slots], rest[slots:]
    out_ref, weights, final, qs, ks, vs, mix = rest
    lon, width = out_ref.shape
    band, frame, shift, level = meta[0], meta[1], meta[2], meta[3]
    parity = lax.rem(frame, 2)
    r1 = width // n_bands
    r3 = 3 * r1

    bands = slot_bands(band, parity, n_bands)
    for group, which in ((mine, parity), (other, 1 - parity)):
        for b, ref in zip(bands, group):
            weights[which, pl.ds(pl.multiple_of(b * r3, 16), r3), :] = ref[:r3, :]
            final[which, pl.ds(pl.multiple_of(b * r1, 16), r1), :] = ref[r3:, :]

    nt = (((1,), (1,)), ((), ()))

    def proj(which, part, x):
        return lax.dot_general(
            weights[which, part * width : (part + 1) * width, :], x, nt, preferred_element_type=F32
        )

    own = normed[0]
    qs[0] = unit_rows(proj(0, 0, own)).astype(BF)
    for j in range(3):
        x = normed[j]
        ks[j] = unit_rows(proj(0, 1, x)).astype(BF)
        vs[j] = proj(0, 2, x).astype(BF)
    kcol = lax.broadcasted_iota(jnp.int32, (lon, 1), 0)
    qcol = lax.broadcasted_iota(jnp.int32, (1, lon), 1)

    def window(col):
        c = col - shift
        c = jnp.where(c < 0, c + lon, c)
        w = jnp.zeros_like(c)
        for edge in range(WINDOW, lon, WINDOW):
            w = w + (c >= edge).astype(jnp.int32)
        return w

    same = window(kcol) == window(qcol)
    side = 1 - 2 * (band % 2)
    biases = []
    for j, off in enumerate((0, side, -side)):
        row = band + off
        exists = (row >= 0) & (row < n_bands)
        limit = jnp.where(exists, tally[jnp.clip(row, 0, n_bands - 1)], 0)
        seen = same & (kcol < limit)
        if j == 0:
            seen = seen | (kcol == qcol)
        biases.append(jnp.where(seen, 0.0, FAR).astype(F32))
    tn = (((0,), (0,)), ((), ()))
    def time_part(i):
        j, part = i // 2, 1 + i % 2
        if j == n_time:
            qs[1] = unit_rows(proj(1, 0, normed[0])).astype(BF)
            return
        out = proj(1, part, normed[j + 2 if j else 0])
        if part == 1:
            ks[3 + j] = unit_rows(out).astype(BF)
        else:
            vs[3 + j] = out.astype(BF)

    todo = 2 * n_time + 1
    pairs = HEADS // 2
    wide = [jnp.concatenate([b, b], axis=1) for b in biases]
    first_half = lax.broadcasted_iota(jnp.int32, (1, 2 * lon), 1) < lon
    blank = jnp.zeros((HEAD_DIM, lon), BF)
    for h in range(pairs):
        lo = 2 * h * HEAD_DIM
        mid = lo + HEAD_DIM
        hi = mid + HEAD_DIM
        base = LOG2E / math.sqrt(HEAD_DIM)
        factor = jnp.where(first_half, scales[0, 2 * h] * base, scales[0, 2 * h + 1] * base)
        q = jnp.concatenate(
            [
                jnp.concatenate([qs[0, lo:mid, :], blank], axis=1),
                jnp.concatenate([blank, qs[0, mid:hi, :]], axis=1),
            ],
            axis=0,
        )
        x = [
            lax.dot_general(ks[j, lo:hi, :], q, tn, preferred_element_type=F32) * factor + wide[j]
            for j in range(3)
        ]
        for i in range(h * todo // pairs, (h + 1) * todo // pairs):
            time_part(i)
        top = jnp.max(jnp.maximum(jnp.maximum(x[0], x[1]), x[2]), axis=0, keepdims=True)
        e = [jnp.exp2(s - top) for s in x]
        inv = 1.0 / jnp.sum(e[0] + e[1] + e[2], axis=0, keepdims=True)
        o = sum(
            jnp.dot(vs[j, lo:hi, :], e[j].astype(BF), preferred_element_type=F32)
            for j in range(3)
        )
        o = o * inv
        mix[0, lo:mid, :] = o[:HEAD_DIM, :lon].astype(BF)
        mix[0, mid:hi, :] = o[HEAD_DIM:, lon:].astype(BF)

    odd = frame % 2
    back = [0, 2, jnp.where(odd == 1, 1, -1), jnp.where(odd == 1, 3, 1), jnp.where(odd == 1, -1, 3)]
    allow = [(b >= 0) & (b <= PRIOR_SNAPSHOTS) & (frame - b >= 0) for b in back]
    shut = [jnp.where(a, 0.0, FAR).astype(F32) for a in allow]
    def by_head(block):
        return block.astype(F32).reshape(HEADS, HEAD_DIM, lon)

    base = LOG2E / math.sqrt(HEAD_DIM)
    factor = jnp.concatenate([jnp.full((1, lon), scales[1, h] * base) for h in range(HEADS)], axis=0)
    q = by_head(qs[1])
    x = [jnp.sum(q * by_head(ks[3 + j]), axis=1) * factor + shut[j] for j in range(n_time)]
    top = functools.reduce(jnp.maximum, x)
    e = [jnp.exp2(s - top) for s in x]
    inv = 1.0 / sum(e)
    o = sum(
        (e[j] * inv).astype(BF).astype(F32)[:, None, :] * by_head(vs[3 + j])
        for j in range(n_time)
    )
    mix[1] = o.reshape(HEADS * HEAD_DIM, lon).astype(BF)

    update = sum(
        lax.dot_general(mix[w], final[w], (((0,), (1,)), ((), ())), preferred_element_type=F32)
        for w in (0, 1)
    )

    def sigma_of(lv):
        power = (jnp.full((1, width), lv, jnp.int32).astype(F32) + 1.0) / total_levels
        return sigma_low * jnp.exp(power * math.log(sigma_high / sigma_low))

    s, s_next = sigma_of(level), sigma_of(level - 1)
    state = late[0].astype(F32)
    fresh = late[1].astype(F32)
    denoised = state / (1.0 + s * s) + s * lax.rsqrt(1.0 + s * s) * update
    stepped = denoised + s_next * (keep_share * (state - denoised) / s + fresh_share * fresh)
    out_ref[...] = jnp.where(level == 0, sigma_high * fresh, stepped).astype(BF)


def body(
    noisy_snapshot_stack,
    gaussian_perturbation,
    snapshot_noise_indices,
    partition_longitude_starts,
    latitude_patch_tally,
    normalizer_scaling,
    head_score_scales,
    local_projection_matrices,
    time_projection_matrices,
    final_projection_matrices,
):
    frames, rows, lon, width = noisy_snapshot_stack.shape
    assert frames == 1 and rows == 1
    n, nf = lax.axis_size("band"), lax.axis_size("frame")
    assert n % 2 == 0 and nf % 2 == 0
    band, frame = lax.axis_index("band"), lax.axis_index("frame")
    parity = frame % 2
    state = noisy_snapshot_stack.reshape(lon, width)
    noise = gaussian_perturbation.reshape(lon, width)

    smem = pl.BlockSpec(memory_space=pltpu.SMEM)
    vmem = pl.BlockSpec(memory_space=pltpu.VMEM)
    hbm = pl.BlockSpec(memory_space=pltpu.HBM)
    chunk_a = jnp.concatenate([local_projection_matrices, final_projection_matrices[:width]], axis=1).T
    chunk_b = jnp.concatenate([time_projection_matrices, final_projection_matrices[width:]], axis=1).T
    own0 = jnp.where(parity == 0, chunk_a, chunk_b)
    own1 = jnp.where(parity == 0, chunk_b, chunk_a)

    meta = jnp.stack(
        [band, frame, partition_longitude_starts[0], snapshot_noise_indices[0]]
    ).astype(jnp.int32)
    ring, core = ring_pairs(nf, n), core_pairs(nf, n)
    half = n // 2
    chain0, chain1 = [own0], [own1]
    partners = exchange_bands(state, 0)
    others = exchange_bands(state, 1)
    two_back = rotate_frame(state, 2)
    for h in range(half):
        a, b = chain0[-1], chain1[-1]
        if h == 1:
            a, meta = lax.optimization_barrier((a, meta))
        chain0.append(lax.ppermute(a, AXES, ring))
        if h < half - 1:
            chain1.append(lax.ppermute(b, AXES, ring))
    swap0 = [lax.ppermute(c, AXES, core) for c in chain0[1:half]]
    swap1 = [lax.ppermute(c, AXES, core) for c in chain1[1:half]]
    swap_last = lax.ppermute(chain0[half], AXES, core)
    mine = chain0 + swap1
    other = chain1 + [swap_last] + swap0
    partner = lax.ppermute(state, AXES, core)
    partner_two = lax.ppermute(two_back, AXES, core)
    past = [two_back, partner, partner_two]
    if nf > 4:
        past.append(rotate_frame(state, 3))

    n_time = 1 + len(past)
    gathered = jnp.stack([state, partners, others, *past])
    normed = pl.pallas_call(
        norm_kernel,
        out_shape=jax.ShapeDtypeStruct(gathered.shape, BF),
        in_specs=[vmem, vmem],
        out_specs=vmem,
        compiler_params=pltpu.CompilerParams(vmem_limit_bytes=8 * 1024 * 1024),
        name="norm",
    )(normalizer_scaling.reshape(1, width), gathered)
    late = jnp.stack([state, noise])
    out = pl.pallas_call(
        functools.partial(kernel, n_time, n, nf),
        out_shape=jax.ShapeDtypeStruct((lon, width), BF),
        in_specs=[smem] * 3 + [vmem] * (2 + 2 * n),
        out_specs=vmem,
        scratch_shapes=[
            pltpu.VMEM((2, 3 * width, width), BF),
            pltpu.VMEM((2, width, width), BF),
            pltpu.VMEM((2, width, lon), BF),
            pltpu.VMEM((3 + n_time, width, lon), BF),
            pltpu.VMEM((3 + n_time, width, lon), BF),
            pltpu.VMEM((2, width, lon), BF),
        ],
        compiler_params=pltpu.CompilerParams(vmem_limit_bytes=20 * 1024 * 1024),
        name="block",
    )(
        meta, head_score_scales, latitude_patch_tally,
        normed, late, *mine, *other,
    )
    return out.reshape(noisy_snapshot_stack.shape)


def solution(mesh):
    return jax.shard_map(
        body,
        mesh=mesh,
        in_specs=(
            P("frame", "band", None, None),
            P("frame", "band", None, None),
            P("frame"),
            P("frame"),
            P(),
            P(),
            P(),
            P(None, "band"),
            P(None, "band"),
            P(None, "band"),
        ),
        out_specs=P("frame", "band", None, None),
        check_vma=False,
    )
```
